512 devices in a mesh: branch: 32 (over z_hi, x, core), fsdp: 16 (over z_lo, y).
Axes of the slice: x: 4, y: 8, z: 8 (z_hi: 4, z_lo: 2; z = z_hi * 2 + z_lo), core: 2. Of those that a mesh axis runs over, the one named last changes fastest.
Arguments:
- activations: bfloat16 [32, 512, 192], P('branch', 'fsdp'), may hold values from -16 to 16
- weights: bfloat16 [32, 192, 29568], P('branch', None, 'fsdp'), may hold values from -6 to 6
- output_grads: bfloat16 [32, 512, 29568], P('branch', None, 'fsdp'), may hold values from -16 to 16
Outputs:
- merged: bfloat16 [192, 29568], P(None, 'fsdp')
- mean_fisher: float32 [192, 29568], P(None, 'fsdp')
The draws below stay inside these ranges and needn't reach their ends.
All inputs are finite; a program needn't handle non-finite values.
Results may differ from the reference program's by a relative error of at most 0.0038.
Values may be sent and summed in bfloat16 or wider, within the bound.
A program may use at most 64 MiB of HBM per device.

```python
import math
import jax
import jax.numpy as jnp
from jax import lax

FF = 29568
ROWS = 192
TOKENS = 512
BRANCHES = 32


def scaled_field(key, width):
    keys = jax.random.split(key, 3)
    groups = 8
    base = jax.random.normal(keys[0], (BRANCHES, TOKENS, width), jnp.float32)
    base = jnp.clip(base, -4.0, 4.0)
    token_scale = jnp.exp(jax.random.uniform(keys[1], (BRANCHES, TOKENS, 1), jnp.float32, math.log(0.2), math.log(2.0)))
    column_scale = jnp.exp(jax.random.uniform(keys[2], (BRANCHES, groups, 1, width), jnp.float32, math.log(0.05), math.log(2.0)))
    grouped = (base * token_scale).reshape(BRANCHES, groups, TOKENS // groups, width) * column_scale
    return grouped.reshape(BRANCHES, TOKENS, width).astype(jnp.bfloat16)


def draw_activations(key, part):
    return scaled_field(jax.random.fold_in(key, 11), ROWS)


def draw_output_grads(key, part):
    return scaled_field(jax.random.fold_in(key, 23), FF)


def block_scale(key, shape, pieces, low, top_value):
    def one(dim, blocks):
        heights = jax.random.uniform(jax.random.fold_in(jax.random.fold_in(key, 6), dim), (blocks,), jnp.float32, low / len(pieces), top_value / len(pieces))
        return jnp.repeat(jnp.exp(heights), shape[dim] // blocks).reshape((-1,) + (1,) * (len(shape) - dim - 1))

    loudness = one(*pieces[0])
    for cut in pieces[1:]:
        loudness = loudness * one(*cut)
    return loudness


def centred(key, shape, scale, bound, pieces=(), kind=jnp.bfloat16):
    level = block_scale(key, shape, pieces, -0.22, 0.18) if pieces else 1.0
    values = jax.random.normal(key, shape, jnp.float32) * scale * level
    return jnp.minimum(jnp.maximum(values, -bound), bound).astype(kind)


def setup_inputs(seed: int = 0) -> dict:
    streams_of = jax.random.split(jax.random.key(seed), 4)
    return {
        "activations": draw_activations(jax.random.fold_in(streams_of[3], 71), 0),
        "weights": centred(streams_of[1], (BRANCHES, ROWS, FF), 1.0, 6.0, ((0, 32), (2, 16))),
        "output_grads": draw_output_grads(jax.random.fold_in(streams_of[3], 71), 0),
    }


def branch_fisher(act_branch, grad_branch):
    act_f = act_branch.astype(jnp.float32)
    act_sq = (act_f * act_f).astype(jnp.bfloat16)
    grad_f = grad_branch.astype(jnp.float32)
    grad_sq = (grad_f * grad_f).astype(jnp.bfloat16)
    fisher = lax.dot_general(act_sq, grad_sq, (((0,), (0,)), ((), ())), preferred_element_type=jnp.float32)
    return fisher / TOKENS


def reference(activations, weights, output_grads):
    def step(carry, items):
        act_branch, w_branch, grad_branch = items
        fisher = branch_fisher(act_branch, grad_branch)
        return (carry[0] + fisher * w_branch.astype(jnp.float32), carry[1] + fisher), None

    start = (jnp.zeros((ROWS, FF), jnp.float32), jnp.zeros((ROWS, FF), jnp.float32))
    totals, unused = lax.scan(step, start, (activations, weights, output_grads))
    total_weighted, total_fisher = totals
    merged = (total_weighted / (total_fisher + 1e-6)).astype(jnp.bfloat16)
    return merged, total_fisher / BRANCHES
```

```python
import functools

import jax
import jax.numpy as jnp
from jax import lax
from jax.experimental import pallas as pl
from jax.experimental.pallas import tpu as pltpu
from jax.sharding import PartitionSpec as P

MESH = pl.DeviceIdType.MESH
F32, BF16 = jnp.float32, jnp.bfloat16
ROWS, FF, TOK, OWN = 192, 1848, 512, 32
FS = TOK // OWN
RX, CZ, HALF = ROWS // 4, 256, 1024
AHEAD = (2, 1, 3, 0)


def kernel(
    act_hbm, w_hbm, g_hbm, mf,
    act_v, g_full, w_full, g_tail, w_tail, g_in, w_in, sq, wt, pack, at,
    acc, snd, rx, zs, zrx,
    load_sem, g_s, g_r, a_s, a_r, f_s, f_r, x_s, x_r, z_s, z_r,
    agz_s, agz_r, agx_s, agx_r, agc_s, agc_r,
):
    b, fs = lax.axis_index("branch"), lax.axis_index("fsdp")
    zh, x, c = b // 8, lax.rem(b // 2, 4), lax.rem(b, 2)
    zl, y = fs // 8, lax.rem(fs, 8)

    def dev(zh=zh, x=x, c=c, fs=fs):
        return (zh * 8 + x * 2 + c, fs)

    other = dev(c=1 - c)
    steps = sorted(((dy, dz) for dy in range(8) for dz in range(2) if dy or dz), key=lambda s: -(min(s[0], 8 - s[0]) + s[1]))
    mates = [lax.rem(zl + dz, 2) * 8 + lax.rem(y + dy, 8) for dy, dz in steps]
    senders = [lax.rem(zl + dz, 2) * 8 + lax.rem(y + 8 - dy, 8) for dy, dz in steps]
    xs = {d: lax.rem(x + d, 4) for d in range(4)}
    zs_to = [lax.rem(zh + d, 4) for d in AHEAD]

    loads = [
        pltpu.make_async_copy(act_hbm.at[0], act_v, load_sem.at[0]),
        pltpu.make_async_copy(g_hbm.at[0], g_full, load_sem.at[1]),
        pltpu.make_async_copy(w_hbm.at[0], w_full, load_sem.at[2]),
    ]
    for cp in loads:
        cp.start()
    barrier = pltpu.get_barrier_semaphore()
    partners = [dev(fs=m) for m in mates] + [other] + [dev(x=xs[d]) for d in (1, 2, 3)] + [dev(zh=q) for q in zs_to[:3]]
    for p in partners:
        pl.semaphore_signal(barrier, inc=1, device_id=p, device_id_type=MESH)

    loads[0].wait()
    a = act_v[...]
    a = a * a
    pack[0, fs, 0:32, :] = a[:, 0:128]
    pack[0, fs, 32:48, 0:64] = a[0:16, 128:192]
    pack[0, fs, 32:48, 64:128] = a[16:32, 128:192]
    loads[1].wait()
    loads[2].wait()
    g_tail[...] = jnp.zeros_like(g_tail)
    w_tail[...] = jnp.zeros_like(w_tail)
    g_tail[:, 0:56] = g_full[:, 1792:1848]
    w_tail[:, 0:56] = w_full[:, 1792:1848]

    pl.semaphore_wait(barrier, len(partners))

    def remote(src, dst, s, r, to):
        return pltpu.make_async_remote_copy(src_ref=src, dst_ref=dst, send_sem=s, recv_sem=r, device_id=to, device_id_type=MESH)

    sent = []
    for i, m in enumerate(mates):
        cp = remote(pack.at[0, fs], pack.at[0, fs], a_s.at[i], a_r.at[i], dev(fs=m))
        cp.start()
        sent.append(cp)

    def push(gs, ws):
        for i in range(2):
            lo, hi = (0, 768) if i == 0 else (768, 1024)
            remote(gs[i], g_in.at[:, lo:hi], g_s.at[i], g_r.at[i], other).start()
            remote(ws[i], w_in.at[:, lo:hi], g_s.at[2 + i], g_r.at[2 + i], other).start()

    @pl.when(c == 0)
    def _():
        push((g_full.at[:, 1024:1792], g_tail), (w_full.at[:, 1024:1792], w_tail))

    @pl.when(c == 1)
    def _():
        push((g_full.at[:, 0:768], g_full.at[:, 768:1024]), (w_full.at[:, 0:768], w_full.at[:, 768:1024]))

    def square(slot, k, g):
        g = g * g
        g = g.reshape(FS, 2, 16, CZ)
        for h in range(2):
            sq[slot, k, 256 * h : 256 * h + 256, :] = g[:, h].reshape(256, CZ)

    for cc in range(2):

        @pl.when(c == cc)
        def _():
            for k in range(4):
                lo = cc * HALF + k * CZ
                if lo + CZ <= FF:
                    square(0, k, g_full[:, lo : lo + CZ])
                    wt[0, k] = w_full[:, lo : lo + CZ]
                else:
                    square(0, k, g_tail[...])
                    wt[0, k] = w_tail[...]

    pushed = []
    for i in range(2):
        lo, hi = (0, 768) if i == 0 else (768, 1024)
        pushed.append(remote(g_in.at[:, lo:hi], g_in.at[:, lo:hi], g_s.at[i], g_r.at[i], other))
        pushed.append(remote(w_in.at[:, lo:hi], w_in.at[:, lo:hi], g_s.at[2 + i], g_r.at[2 + i], other))
    for cp in pushed:
        cp.wait_recv()
    for k in range(4):
        square(1, k, g_in[:, k * CZ : (k + 1) * CZ])
        wt[1, k] = w_in[:, k * CZ : (k + 1) * CZ]

    fwd = []

    def pass_on(i, blk):
        cp = remote(pack.at[0, blk], pack.at[1, blk], f_s.at[i], f_r.at[i], other)
        cp.start()
        fwd.append(cp)

    pass_on(15, fs)
    for i in reversed(range(15)):
        sent[i].wait_recv()
        pass_on(i, senders[i])

    def turn(slot):
        p = pack[slot]
        left = jnp.concatenate([p[:, 0:16].reshape(256, 128), p[:, 16:32].reshape(256, 128)], axis=0)
        at[slot, 0:128, :] = left.T
        right = p[:, 32:48].reshape(256, 128).T
        at[slot, 128:192, 0:256] = right[0:64]
        at[slot, 128:192, 256:512] = right[64:128]

    turn(0)
    for cp in fwd:
        cp.wait_recv()
    turn(1)

    xcopies = []
    for j in range(4):
        k = zs_to[j]
        f0 = jnp.dot(at[0], sq[0, k], preferred_element_type=F32)
        f1 = jnp.dot(at[1], sq[1, k], preferred_element_type=F32)
        tf = f0 + f1
        tw = f0 * wt[0, k].astype(F32) + f1 * wt[1, k].astype(F32)
        for r in range(4):
            rows = slice(r * RX, r * RX + RX)
            acc[j, r, 0], acc[j, r, 1] = tf[rows], tw[rows]
            snd[j, r, 0], snd[j, r, 1] = tf[rows].astype(BF16), tw[rows].astype(BF16)
        row = []
        for d in (2, 1, 3):
            cp = remote(snd.at[j, xs[d]], rx.at[j, d - 1], x_s.at[j, d - 1], x_r.at[j, d - 1], dev(x=xs[d]))
            cp.start()
            row.append(cp)
        xcopies.append(row)

    zcopies = []
    for j in range(4):
        for cp in xcopies[j]:
            cp.wait_recv()
        s = acc[j, x] + rx[j, 0].astype(F32) + rx[j, 1].astype(F32) + rx[j, 2].astype(F32)
        if j < 3:
            zs[j] = s.astype(BF16)
            cp = remote(zs.at[j], zrx.at[j], z_s.at[j], z_r.at[j], dev(zh=zs_to[j]))
            cp.start()
            zcopies.append(cp)
    for j in (1, 2, 0):
        zcopies[j].wait_recv()
        s = s + zrx[j].astype(F32)
    s = s * (1.0 / TOK)
    tf, tw = s[0], s[1]

    def block(x, zh, c=c):
        return mf.at[:, pl.ds(pl.multiple_of(x * RX, 16), RX), pl.ds(pl.multiple_of(c * HALF + zh * CZ, CZ), CZ)]

    own = block(x, zh)
    own[0] = (tw / (tf + 1e-6)).astype(BF16)
    own[1] = (tf * (1.0 / 32)).astype(BF16)

    agz, agx, agc = [], {}, []

    def along_x(j, z):
        for d in (2, 1, 3):
            blk = block(x, z)
            cp = remote(blk, blk, agx_s.at[j, d - 1], agx_r.at[j, d - 1], dev(x=xs[d]))
            cp.start()
            agx[j, d] = cp

    def across(xx, z):
        i = len(agc)
        blk = block(xx, z)
        cp = remote(blk, blk, agc_s.at[i], agc_r.at[i], other)
        cp.start()
        agc.append(cp)

    for j in range(3):
        cp = remote(own, own, agz_s.at[j], agz_r.at[j], dev(zh=zs_to[j]))
        cp.start()
        agz.append(cp)
    along_x(3, zh)
    across(x, zh)
    zfrom = {j: lax.rem(zh + 4 - AHEAD[j], 4) for j in range(4)}
    for j in (1, 2, 0):
        agz[j].wait_recv()
        along_x(j, zfrom[j])
        across(x, zfrom[j])
    for j in (3, 1, 2, 0):
        for d in (1, 3, 2):
            agx[j, d].wait_recv()
            across(lax.rem(x + 4 - d, 4), zfrom[j])
    for cp in agc:
        cp.wait_recv()
    for cp in sent + pushed + fwd + sum(xcopies, []) + zcopies + agz + list(agx.values()) + agc:
        cp.wait_send()


def on_device(activations, weights, output_grads):
    dma = pltpu.SemaphoreType.DMA
    mf = pl.pallas_call(
        kernel,
        out_shape=jax.ShapeDtypeStruct((2, ROWS, 2 * HALF), BF16),
        in_specs=[pl.BlockSpec(memory_space=pl.ANY)] * 3,
        out_specs=pl.BlockSpec(memory_space=pltpu.VMEM),
        scratch_shapes=[
            pltpu.VMEM((OWN, ROWS), BF16),
            pltpu.VMEM((TOK, FF), BF16),
            pltpu.VMEM((ROWS, FF), BF16),
            pltpu.VMEM((TOK, CZ), BF16),
            pltpu.VMEM((ROWS, CZ), BF16),
            pltpu.VMEM((TOK, HALF), BF16),
            pltpu.VMEM((ROWS, HALF), BF16),
            pltpu.VMEM((2, 4, TOK, CZ), BF16),
            pltpu.VMEM((2, 4, ROWS, CZ), BF16),
            pltpu.VMEM((2, FS, 48, 128), BF16),
            pltpu.VMEM((2, ROWS, TOK), BF16),
            pltpu.VMEM((4, 4, 2, RX, CZ), F32),
            pltpu.VMEM((4, 4, 2, RX, CZ), BF16),
            pltpu.VMEM((4, 3, 2, RX, CZ), BF16),
            pltpu.VMEM((3, 2, RX, CZ), BF16),
            pltpu.VMEM((3, 2, RX, CZ), BF16),
            dma((3,)), dma((4,)), dma((4,)), dma((15,)), dma((15,)), dma((16,)), dma((16,)),
            dma((4, 3)), dma((4, 3)), dma((3,)), dma((3,)),
            dma((3,)), dma((3,)), dma((4, 3)), dma((4, 3)), dma((16,)), dma((16,)),
        ],
        compiler_params=pltpu.CompilerParams(collective_id=0, has_side_effects=True, vmem_limit_bytes=40 << 20),
        name="merge",
    )(activations, weights, output_grads)
    return mf[0, :, :FF], mf[1, :, :FF].astype(F32)


def solution(mesh):
    placed = (P("branch", "fsdp", None), P("branch", None, "fsdp"), P("branch", None, "fsdp"))
    return jax.shard_map(
        on_device, mesh=mesh, in_specs=placed, out_specs=(P(None, "fsdp"), P(None, "fsdp")), check_vma=False
    )
```
